256 devices in a mesh: dp: 32 (over z_lo, y, core), shard: 8 (over x, z_hi).
Axes of the slice: x: 4, y: 4, z: 8 (z_hi: 2, z_lo: 4; z = z_hi * 4 + z_lo), core: 2. Of those that a mesh axis runs over, the one named last changes fastest.
Arguments:
- inputs: bfloat16 [32768, 8192], P(('dp', 'shard')), may hold values from -6 to 6
- grad_out: bfloat16 [32768, 1024], P(('dp', 'shard')), may hold values from -6 to 6
- weight: bfloat16 [8192, 1024], P('shard'), may hold values from -0.1875 to 0.1875
- projector: bfloat16 [8192, 512], P('shard'), may hold values from -0.0625 to 0.0625
- first_moment: float32 [512, 1024], P('dp'), may hold values from -320 to 320
- second_moment: float32 [512, 1024], P('dp'), may hold values from 8192 to 131072
Outputs:
- input_grad: bfloat16 [32768, 8192], P(('dp', 'shard'))
- weight_update: float32 [8192, 1024], P('shard')
- new_first: float32 [512, 1024], P('dp')
- new_second: float32 [512, 1024], P('dp')
The draws below stay inside these ranges and needn't reach their ends.
All inputs are finite; a program needn't handle non-finite values.
Results may differ from the reference program's by a relative error of at most 0.009.
Values may be sent and summed in bfloat16 or wider, within the bound.
No kernel may reach another device: no remote copies, remote signals or barrier semaphores. Data moves between devices by JAX's collectives and lax.ppermute only.
A program may use at most 128 MiB of HBM per device.

```python
import math
import jax
import jax.numpy as jnp
from jax import lax

D = 8192
KV = 1024
R = 512
TOKENS = 32768


def steps_of(key, dims, shards, low, top_value):
    gain = 1.0
    for position, blocks in shards:
        heights = jax.random.uniform(jax.random.fold_in(jax.random.fold_in(key, 6), position), (blocks,), jnp.float32, low / len(shards), top_value / len(shards))
        gain = gain * jnp.repeat(jnp.exp(heights), dims[position] // blocks).reshape((-1,) + (1,) * (len(dims) - 1 - position))
    return gain


def scatter_about(own_key, extent, width, bound, cuts=(), held_as=jnp.bfloat16):
    values = width * jax.random.normal(own_key, extent, jnp.float32)
    if cuts:
        values = values * steps_of(own_key, extent, cuts, -0.22, 0.18)
    return jnp.clip(values, -bound, bound).astype(held_as)


def setup_inputs(seed: int = 0) -> dict:
    keys = jax.random.split(jax.random.key(seed), 7)
    return {
        "inputs": scatter_about(keys[0], (TOKENS, D), 1.0, 6.0, ((0, 256),)),
        "grad_out": scatter_about(keys[1], (TOKENS, KV), 1.0, 6.0, ((0, 256),)),
        "weight": scatter_about(keys[2], (D, KV), KV ** -0.5, 0.1875, ((0, 8),)),
        "projector": scatter_about(keys[3], (D, R), D ** -0.5, 0.0625, ((0, 8),)),
        "first_moment": scatter_about(keys[4], (R, KV), (0.3 * TOKENS ** 0.5), 320.0, ((0, 32),), jnp.float32),
        "second_moment": jnp.clip(jnp.exp(math.log(131072.0) - 2.7725887 * jax.random.uniform(keys[5], (R, KV), jnp.float32) ** steps_of(keys[5], (R, KV), ((0, 32),), -0.2, 0.2)), 8192.0, 131072.0),
    }


beta_one = 0.9
beta_two = 0.999
bias_one = 0.999973438601112
bias_two = 0.0952078528862904
epsilon = 1e-08

def widen(values):
    return values.astype(jnp.float32)

def reference(inputs, grad_out, weight, projector, first_moment, second_moment):
    input_grad = jnp.dot(widen(grad_out), widen(weight).T, preferred_element_type=jnp.float32).astype(jnp.bfloat16)
    projected_inputs = jnp.dot(widen(inputs), widen(projector), preferred_element_type=jnp.float32)
    projected_grad = jnp.dot(projected_inputs.T, widen(grad_out), precision=lax.Precision.HIGHEST)
    new_first = beta_one * first_moment + (1.0 - beta_one) * projected_grad
    new_second = beta_two * second_moment + (1.0 - beta_two) * projected_grad * projected_grad
    direction = (new_first / bias_one / (jnp.sqrt(new_second / bias_two) + epsilon)).astype(jnp.bfloat16)
    weight_update = jnp.dot(widen(projector), widen(direction), preferred_element_type=jnp.float32)
    return (input_grad, weight_update, new_first, new_second)
```

```python
import itertools

import jax
import jax.numpy as jnp
from jax import lax
from jax.sharding import Mesh
from jax.sharding import PartitionSpec as P

beta_one = 0.9
beta_two = 0.999
bias_one = 0.999973438601112
bias_two = 0.0952078528862904
epsilon = 1e-08

NAMES = ("zl", "y", "c", "x", "zh")
SIZES = {"zl": 4, "y": 4, "c": 2, "x": 4, "zh": 2}
DP = ("zl", "y", "c")
SHARD = ("x", "zh")
WIDE = jnp.float32
NARROW = jnp.bfloat16


def send(value, **shift):
    axes = tuple(name for name in NAMES if name in shift)
    sizes = [SIZES[name] for name in axes]
    flat = {at: i for i, at in enumerate(itertools.product(*map(range, sizes)))}
    pairs = [
        (i, flat[tuple((p + shift[n]) % s for p, n, s in zip(at, axes, sizes))])
        for at, i in flat.items()
    ]
    return lax.ppermute(value, axes, pairs)


def adam_step(projected_grad, first_moment, second_moment):
    new_first = beta_one * first_moment + (1.0 - beta_one) * projected_grad
    new_second = beta_two * second_moment + (1.0 - beta_two) * projected_grad * projected_grad
    direction = new_first / bias_one / (jnp.sqrt(new_second / bias_two) + epsilon)
    return (new_first, new_second, direction.astype(NARROW))


def dot(a, b, contract):
    return lax.dot_general(a, b, ((contract[:1], contract[1:]), ((), ())), preferred_element_type=WIDE)


def slot_permutation():
    row = lax.broadcasted_iota(jnp.int32, (512, 512), 0)
    slot = lax.broadcasted_iota(jnp.int32, (512, 512), 1)
    cc, dy, dz, low = slot // 256, slot // 64 % 4, slot // 16 % 4, slot % 16
    zl = (lax.axis_index("zl") + dz) % 4
    y = (lax.axis_index("y") + dy) % 4
    c = (lax.axis_index("c") + cc) % 2
    return (row == ((zl * 4 + y) * 2 + c) * 16 + low).astype(NARROW)


def fold(slots, axis):
    rows = slots.shape[0] // 4
    total = slots[:rows].astype(WIDE)
    for s in (1, 2, 3):
        total = total + send(slots[rows * s : rows * s + rows], **{axis: s}).astype(WIDE)
    return total


def spread(own, axis):
    return jnp.concatenate([own] + [send(own, **{axis: -s}) for s in (1, 2, 3)], 0)


def swap_shard(mine):
    half = mine.shape[0] // 2
    c, zh = lax.axis_index("c"), lax.axis_index("zh")
    part = send(lax.dynamic_slice_in_dim(mine, c * half, half, 0), zh=1)
    other = send(part, c=1)
    both = jnp.zeros((4 * half, mine.shape[1]), mine.dtype)
    both = lax.dynamic_update_slice_in_dim(both, mine, zh * 2 * half, 0)
    both = lax.dynamic_update_slice_in_dim(both, part, (1 - zh) * 2 * half + c * half, 0)
    return lax.dynamic_update_slice_in_dim(both, other, (1 - zh) * 2 * half + (1 - c) * half, 0)


def body(inputs, grad_out, weight, projector, first_moment, second_moment):
    x = lax.axis_index("x")

    columns = [lax.dynamic_slice_in_dim(inputs, (x + s) % 4 * 2048, 2048, 1) for s in range(4)]
    tokens = [columns[0]] + [send(columns[s], x=s) for s in (1, 2, 3)]
    grads = [grad_out] + [send(grad_out, x=s) for s in (1, 2, 3)]
    tokens = jnp.concatenate(tokens, 0)
    grads = jnp.concatenate(grads, 0)

    order = slot_permutation()
    basis = swap_shard(projector)
    basis = dot(basis, order, (1, 0)).astype(NARROW)
    own_basis = dot(projector, order, (1, 0)).astype(NARROW)

    projected = dot(tokens, basis, (1, 0)).astype(NARROW)
    partial = dot(projected, grads, (0, 0))

    kept = partial[:256] + send(partial[256:].astype(NARROW), c=1).astype(WIDE)
    kept = fold(kept.astype(NARROW), "y")
    kept = fold(kept.astype(NARROW), "zl")
    kept = kept + send(kept, zh=1)
    far = [send(kept, x=s) for s in (1, 2, 3)]
    projected_grad = (kept + far[1]) + (far[0] + far[2])

    new_first, new_second, direction = adam_step(projected_grad, first_moment, second_moment)

    near = spread(spread(direction, "zl"), "y")
    far = send(near, c=1)
    weight_update = dot(own_basis, jnp.concatenate([near, far], 0), (1, 0))

    both = swap_shard(weight)
    block = dot(grads, both, (1, 1)).astype(NARROW)
    input_grad = jnp.zeros(inputs.shape, NARROW)
    for s in range(4):
        part = block[128 * s : 128 * s + 128]
        part = send(part, x=-s) if s else part
        input_grad = lax.dynamic_update_slice_in_dim(input_grad, part, (x + s) % 4 * 2048, 1)
    return (input_grad, weight_update, new_first, new_second)


def solution(mesh):
    fine = Mesh(mesh.devices.reshape([SIZES[name] for name in NAMES]), NAMES)
    return jax.shard_map(
        body,
        mesh=fine,
        in_specs=(
            P(DP + SHARD, None),
            P(DP + SHARD, None),
            P(SHARD, None),
            P(SHARD, None),
            P(DP, None),
            P(DP, None),
        ),
        out_specs=(P(DP + SHARD, None), P(SHARD, None), P(DP, None), P(DP, None)),
        check_vma=False,
    )
```

```python
import functools
import itertools

import jax
import jax.numpy as jnp
from jax import lax
from jax.experimental import pallas as pl
from jax.experimental.pallas import tpu as pltpu
from jax.sharding import Mesh
from jax.sharding import PartitionSpec as P

beta_one = 0.9
beta_two = 0.999
bias_one = 0.999973438601112
bias_two = 0.0952078528862904
epsilon = 1e-08

NAMES = ("zl", "y", "c", "x", "zh")
SIZES = {"zl": 4, "y": 4, "c": 2, "x": 4, "zh": 2}
DP = ("zl", "y", "c")
SHARD = ("x", "zh")
WIDE = jnp.float32
NARROW = jnp.bfloat16


def send(value, **shift):
    axes = tuple(name for name in NAMES if name in shift)
    sizes = [SIZES[name] for name in axes]
    flat = {at: i for i, at in enumerate(itertools.product(*map(range, sizes)))}
    pairs = [
        (i, flat[tuple((p + shift[n]) % s for p, n, s in zip(at, axes, sizes))])
        for at, i in flat.items()
    ]
    return lax.ppermute(value, axes, pairs)


def adam_step(projected_grad, first_moment, second_moment):
    new_first = beta_one * first_moment + (1.0 - beta_one) * projected_grad
    new_second = beta_two * second_moment + (1.0 - beta_two) * projected_grad * projected_grad
    direction = new_first / bias_one / (jnp.sqrt(new_second / bias_two) + epsilon)
    return (new_first, new_second, direction.astype(NARROW))


def dot(a, b, contract):
    return lax.dot_general(a, b, ((contract[:1], contract[1:]), ((), ())), preferred_element_type=WIDE)


def slot_permutation(turned):
    row = lax.broadcasted_iota(jnp.int32, (512, 512), 0)
    slot = lax.broadcasted_iota(jnp.int32, (512, 512), 1)
    cc, dy, dz, low = slot // 256, slot // 64 % 4, slot // 16 % 4, slot % 16
    zl = (lax.axis_index("zl") + dz) % 4 if turned else dz
    y = (lax.axis_index("y") + dy) % 4
    c = (lax.axis_index("c") + cc) % 2
    return (row == ((zl * 4 + y) * 2 + c) * 16 + low).astype(NARROW)


def fold(slots, axis):
    rows = slots.shape[0] // 4
    total = slots[:rows].astype(WIDE)
    for s in (1, 2, 3):
        total = total + send(slots[rows * s : rows * s + rows], **{axis: s}).astype(WIDE)
    return total


def spread(own, axis):
    return join([own] + [send(own, **{axis: -s}) for s in (1, 2, 3)])


def after(value, *others):
    return lax.optimization_barrier((value,) + others)[0]


def join(parts):
    rows, low = parts[0].shape[0], jnp.array(-jnp.inf, parts[0].dtype)
    padded = [
        lax.pad(part, low, ((i * rows, (len(parts) - 1 - i) * rows, 0), (0, 0, 0)))
        for i, part in enumerate(parts)
    ]
    return functools.reduce(jnp.maximum, padded)


def share_of(mine, ways):
    rows = mine.shape[0] // 2 // ways
    at = (lax.axis_index("c") * ways + lax.axis_index("y") % ways) * rows
    return lax.dynamic_slice_in_dim(mine, at, rows, 0)


def assemble(mine, part, other):
    half = part.shape[0]
    c, zh = lax.axis_index("c"), lax.axis_index("zh")
    both = jnp.zeros((4 * half, mine.shape[1]), mine.dtype)
    both = lax.dynamic_update_slice_in_dim(both, mine, zh * 2 * half, 0)
    both = lax.dynamic_update_slice_in_dim(both, part, (1 - zh) * 2 * half + c * half, 0)
    return lax.dynamic_update_slice_in_dim(both, other, (1 - zh) * 2 * half + (1 - c) * half, 0)


def place_kernel(*refs):
    blocks, out = refs[:4], refs[4]
    c, x, y, zh = (lax.axis_index(name) for name in ("c", "x", "y", "zh"))
    for s, block in enumerate(blocks):
        base = lax.rem(x + s, 4) * 2048
        other = base + (1 - zh) * 1024
        spots = [(0, 1024, base + zh * 1024)]
        for cc, dy in itertools.product(range(2), range(4)):
            to = other + lax.rem(c + cc, 2) * 512 + lax.rem(y + dy, 4) * 128
            spots.append((1024 + (cc * 4 + dy) * 128, 128, to))
        for at, size, to in spots:
            out[:, pl.ds(pl.multiple_of(to, 128), size)] = block[:, at : at + size]


def place(blocks):
    return pl.pallas_call(
        place_kernel,
        out_shape=jax.ShapeDtypeStruct((128, 8192), NARROW),
        in_specs=[pl.BlockSpec(memory_space=pltpu.VMEM)] * 4,
        out_specs=pl.BlockSpec(memory_space=pltpu.VMEM),
        cost_estimate=pl.CostEstimate(flops=0, bytes_accessed=4 << 20, transcendentals=0),
        compiler_params=pltpu.CompilerParams(vmem_limit_bytes=16 << 20),
    )(*blocks)


def pair(value):
    return lax.ppermute(value, "y", [(0, 1), (1, 0), (2, 3), (3, 2)])


def body(inputs, grad_out, weight, projector, first_moment, second_moment):
    x, y = lax.axis_index("x"), lax.axis_index("y")

    columns = [lax.dynamic_slice_in_dim(inputs, (x + s) % 4 * 2048, 2048, 1) for s in range(4)]
    cut = [jnp.concatenate([columns[s], grad_out], 1) for s in (1, 2, 3)]
    cut = lax.optimization_barrier((*cut, share_of(projector, 2)))
    tokens = {0: columns[0]}
    grads = {0: grad_out}
    for s in (1, 3, 2):
        both = send(cut[s - 1], x=s)
        tokens[s], grads[s] = both[:, :2048], both[:, 2048:]

    basis_part = send(cut[3], zh=1)
    weight_part = send(after(share_of(weight, 4), basis_part), zh=1)
    basis_pair = pair(basis_part)
    odd = y % 2 == 1
    basis_part = jnp.concatenate(
        [jnp.where(odd, basis_pair, basis_part), jnp.where(odd, basis_part, basis_pair)], 0
    )
    basis = assemble(projector, basis_part, send(basis_part, c=1))
    basis = dot(basis, slot_permutation(False), (1, 0)).astype(NARROW)
    own_basis = dot(projector, slot_permutation(True), (1, 0)).astype(NARROW)

    turn = (0, 1, 3, 2)
    projected = {s: dot(tokens[s], basis, (1, 0)).astype(NARROW) for s in turn}
    projected[2], weight_part = lax.optimization_barrier((projected[2], weight_part))
    far = sum(dot(projected[s][:, 256:], grads[s], (0, 0)) for s in turn)
    near = sum(dot(projected[s][:, :256], grads[s], (0, 0)) for s in turn)

    kept = near + send(far.astype(NARROW), c=1).astype(WIDE)
    weight_part = spread(weight_part, "y")
    kept, weight_part = lax.optimization_barrier((kept.astype(NARROW), weight_part))

    weight_other = send(weight_part, c=1)
    all_grads = after(join([grads[s] for s in range(4)]), kept)
    parts = [dot(all_grads, w, (1, 1)).astype(NARROW) for w in (weight, weight_part, weight_other)]
    home = [jnp.concatenate([part[128 * s : 128 * s + 128] for part in parts], 1) for s in range(4)]

    kept = fold(kept, "y").astype(NARROW)
    kept = after(kept, *home).reshape(4, 1, 16, 1024)
    kept = jnp.broadcast_to(kept, (4, 2, 16, 1024)).reshape(8, 16, 1024)
    kept = lax.all_to_all(kept, ("zl", "zh"), 0, 0, tiled=True).astype(WIDE).sum(0)

    home[1] = send(home[1], x=-1)
    home[3] = send(home[3], x=-3)
    kept = after(kept, home[1], home[3])
    away = {s: send(kept, x=s) for s in (1, 3, 2)}
    projected_grad = (kept + away[2]) + (away[1] + away[3])
    home[2] = send(after(home[2], projected_grad), x=-2)

    new_first, new_second, direction = adam_step(projected_grad, first_moment, second_moment)

    rows = spread(direction, "zl")
    rows = spread(rows, "y")
    rows = after(join([rows, send(rows, c=1)]), *home)
    input_grad = place(home)
    weight_update = dot(own_basis, rows, (1, 0))
    return (input_grad, weight_update, new_first, new_second)


def solution(mesh):
    fine = Mesh(mesh.devices.reshape([SIZES[name] for name in NAMES]), NAMES)
    return jax.shard_map(
        body,
        mesh=fine,
        in_specs=(
            P(DP + SHARD, None),
            P(DP + SHARD, None),
            P(SHARD, None),
            P(SHARD, None),
            P(DP, None),
            P(DP, None),
        ),
        out_specs=(P(DP + SHARD, None), P(SHARD, None), P(DP, None), P(DP, None)),
        check_vma=False,
    )
```

```python
import functools
import itertools

import jax
import jax.numpy as jnp
from jax import lax
from jax.experimental import pallas as pl
from jax.experimental.pallas import tpu as pltpu
from jax.sharding import Mesh
from jax.sharding import PartitionSpec as P

beta_one = 0.9
beta_two = 0.999
bias_one = 0.999973438601112
bias_two = 0.0952078528862904
epsilon = 1e-08

NAMES = ("zl", "y", "c", "x", "zh")
SIZES = {"zl": 4, "y": 4, "c": 2, "x": 4, "zh": 2}
DP = ("zl", "y", "c")
SHARD = ("x", "zh")
WIDE = jnp.float32
NARROW = jnp.bfloat16


def send(value, **shift):
    axes = tuple(name for name in NAMES if name in shift)
    sizes = [SIZES[name] for name in axes]
    flat = {at: i for i, at in enumerate(itertools.product(*map(range, sizes)))}
    pairs = [
        (i, flat[tuple((p + shift[n]) % s for p, n, s in zip(at, axes, sizes))])
        for at, i in flat.items()
    ]
    return lax.ppermute(value, axes, pairs)


def adam_step(projected_grad, first_moment, second_moment):
    new_first = beta_one * first_moment + (1.0 - beta_one) * projected_grad
    new_second = beta_two * second_moment + (1.0 - beta_two) * projected_grad * projected_grad
    direction = new_first / bias_one / (jnp.sqrt(new_second / bias_two) + epsilon)
    return (new_first, new_second, direction.astype(NARROW))


def dot(a, b, contract):
    return lax.dot_general(a, b, ((contract[:1], contract[1:]), ((), ())), preferred_element_type=WIDE)


def owner_row(slot, turned):
    cc, dy, dz, low = slot >> 8, (slot >> 6) & 3, (slot >> 4) & 3, slot & 15
    zl = (lax.axis_index("zl") + dz) & 3 if turned else dz
    y = (lax.axis_index("y") + dy) & 3
    c = (lax.axis_index("c") + cc) & 1
    return ((zl * 4 + y) * 2 + c) * 16 + low


def fold(slots, axis, *others):
    rows = slots.shape[0] // 4
    came = [send(slots[rows * s : rows * s + rows], **{axis: s}) for s in (1, 2, 3)]
    came = lax.optimization_barrier((*came, *others))[:3]
    total = slots[:rows].astype(WIDE)
    for part in came:
        total = total + part.astype(WIDE)
    return total


def spread(own, axis):
    return join([own] + [send(own, **{axis: -s}) for s in (1, 2, 3)])


def after(value, *others):
    return lax.optimization_barrier((value,) + others)[0]


def join(parts):
    rows, low = parts[0].shape[0], jnp.array(-jnp.inf, parts[0].dtype)
    padded = [
        lax.pad(part, low, ((i * rows, (len(parts) - 1 - i) * rows, 0), (0, 0, 0)))
        for i, part in enumerate(parts)
    ]
    return functools.reduce(jnp.maximum, padded)


def share_of(mine, ways):
    rows = mine.shape[0] // 2 // ways
    at = (lax.axis_index("c") * ways + lax.axis_index("y") % ways) * rows
    return lax.dynamic_slice_in_dim(mine, at, rows, 0)


def call(kernel, outs, flops, moved, scratch=(), **more):
    return pl.pallas_call(
        kernel,
        out_shape=[jax.ShapeDtypeStruct(*out) for out in outs],
        scratch_shapes=[pltpu.VMEM(*space) for space in scratch],
        cost_estimate=pl.CostEstimate(flops=flops, bytes_accessed=moved, transcendentals=0),
        compiler_params=pltpu.CompilerParams(vmem_limit_bytes=24 << 20),
        **more,
    )


def basis_kernel(mine, part, far, out):
    c, zh = lax.axis_index("c"), lax.axis_index("zh")
    slot = lax.broadcasted_iota(jnp.int32, (512, 1), 0)
    row = lax.broadcasted_iota(jnp.int32, (512, 512), 1)
    order = (row == owner_row(slot, False)).astype(WIDE).astype(NARROW)
    other = (1 - zh) * 1024
    pieces = [(mine[low : low + 256, :], zh * 1024 + low) for low in range(0, 1024, 256)]
    for some, at in ((part, other + c * 512), (far, other + (1 - c) * 512)):
        pieces += [(some[:, :512], at), (some[:, 512:], at + 256)]
    for some, at in pieces:
        moved = dot(order, some, (1, 1)).astype(NARROW)
        out[:, pl.ds(pl.multiple_of(at, 256), 256)] = moved


def project_kernel(x0, g0, xg1, xg2, xg3, basis, far, near, grads, tokens, projected):
    tokens[0:128] = x0[...]
    grads[0:128] = g0[...]
    for s, both in ((1, xg1), (2, xg2), (3, xg3)):
        tokens[128 * s : 128 * s + 128] = both[:, :2048]
        grads[128 * s : 128 * s + 128] = both[:, 2048:]
    for low in range(0, 512, 256):
        some = tokens[low : low + 256, :]
        projected[:, low : low + 256] = dot(basis[...], some, (1, 1)).astype(NARROW)
    far[...] = dot(projected[256:, :], grads[...], (1, 0)).astype(NARROW)
    near[...] = dot(projected[:256, :], grads[...], (1, 0))


def home_kernel(grads, weight, part, other, out):
    x = lax.axis_index("x")
    at = 0
    for some in (weight, part, other):
        for low in range(0, some.shape[0], 256):
            block = dot(grads[...], some[low : low + 256, :], (1, 1)).astype(NARROW)
            for s in range(4):
                out[lax.rem(x + 4 - s, 4), :, at : at + 256] = block[128 * s : 128 * s + 128]
            at += 256


def update_kernel(basis, near, far, out):
    out[...] = dot(basis[:, :256], near[...], (1, 0)) + dot(basis[:, 256:], far[...], (1, 0))


def place_kernel(blocks, out):
    c, y, zh = (lax.axis_index(name) for name in ("c", "y", "zh"))
    other = (1 - zh) * 1024
    spots = [(0, 1024, zh * 1024)]
    for cc, dy in itertools.product(range(2), range(4)):
        to = other + lax.rem(c + cc, 2) * 512 + lax.rem(y + dy, 4) * 128
        spots.append((1024 + (cc * 4 + dy) * 128, 128, to))
    for s in range(4):
        for at, size, to in spots:
            out[:, pl.ds(pl.multiple_of(2048 * s + to, 128), size)] = blocks[s, :, at : at + size]


def body(inputs, grad_out, weight, projector, first_moment, second_moment):
    x = lax.axis_index("x")

    columns = [lax.dynamic_slice_in_dim(inputs, (x + s) % 4 * 2048, 2048, 1) for s in range(4)]
    cut = [jnp.concatenate([columns[s], grad_out], 1) for s in (1, 2, 3)]
    basis_part = share_of(projector, 1)
    basis_part = jnp.concatenate([basis_part[:256], basis_part[256:]], 1)
    rows = jnp.concatenate([basis_part, share_of(weight, 4)], 0)
    cut = lax.optimization_barrier((*cut, rows))
    met = {s: send(cut[s - 1], x=s) for s in (1, 3, 2)}

    rows = send(cut[3], zh=1)
    basis_part, weight_part = rows[:256], rows[256:]
    (basis,) = call(basis_kernel, [((512, 2048), NARROW)], 1 << 20, 1 << 20)(
        projector, basis_part, send(basis_part, c=1)
    )
    quarters = [weight_part] + [send(weight_part, y=-s) for s in (1, 2, 3)]

    far, near, grads = call(
        project_kernel,
        [((256, 1024), NARROW), ((256, 1024), WIDE), ((512, 1024), NARROW)],
        4 << 30,
        10 << 20,
        [((512, 2048), NARROW), ((512, 512), NARROW)],
    )(columns[0], grad_out, met[1], met[2], met[3], basis)

    kept = near + send(far, c=1).astype(WIDE)
    kept = kept.astype(NARROW)

    kept = fold(kept, "y").astype(NARROW)
    kept = jnp.broadcast_to(kept.reshape(4, 1, 16, 1024), (4, 2, 16, 1024)).reshape(8, 16, 1024)
    kept = lax.all_to_all(kept, ("zl", "zh"), 0, 0, tiled=True)
    kept, *quarters = lax.optimization_barrier((kept, *quarters))
    kept = kept.astype(WIDE).sum(0)

    weight_part = join(quarters)
    weight_other = send(weight_part, c=1)
    (home,) = call(home_kernel, [((4, 128, 2048), NARROW)], 2 << 30, 8 << 20)(
        grads, weight, weight_part, weight_other
    )

    away = [send(kept, x=s) for s in (1, 3, 2)]
    *away, home = lax.optimization_barrier((*away, home))
    projected_grad = (kept + away[2]) + (away[0] + away[1])
    home, projected_grad = lax.optimization_barrier((home, projected_grad))
    home = lax.all_to_all(home, "x", 0, 0, tiled=True)

    new_first, new_second, direction = adam_step(projected_grad, first_moment, second_moment)

    slot = lax.broadcasted_iota(jnp.int32, (512, 512), 1)
    row = lax.broadcasted_iota(jnp.int32, (512, 512), 0)
    order = (row == owner_row(slot, True)).astype(NARROW)
    own_basis = dot(projector, order, (1, 0)).astype(NARROW)
    near = after(spread(spread(direction, "zl"), "y"), own_basis, home)
    far = send(near, c=1)
    (input_grad,) = call(place_kernel, [((128, 8192), NARROW)], 1 << 20, 4 << 20)(home)
    (weight_update,) = call(
        update_kernel,
        [((1024, 1024), WIDE)],
        1 << 30,
        6 << 20,
        grid=(4,),
        in_specs=[
            pl.BlockSpec((256, 512), lambda i: (i, 0)),
            pl.BlockSpec((256, 1024), lambda i: (0, 0)),
            pl.BlockSpec((256, 1024), lambda i: (0, 0)),
        ],
        out_specs=[pl.BlockSpec((256, 1024), lambda i: (i, 0))],
    )(own_basis, near, far)
    return (input_grad, weight_update, new_first, new_second)


def solution(mesh):
    fine = Mesh(mesh.devices.reshape([SIZES[name] for name in NAMES]), NAMES)
    return jax.shard_map(
        body,
        mesh=fine,
        in_specs=(
            P(DP + SHARD, None),
            P(DP + SHARD, None),
            P(SHARD, None),
            P(SHARD, None),
            P(DP, None),
            P(DP, None),
        ),
        out_specs=(P(DP + SHARD, None), P(SHARD, None), P(DP, None), P(DP, None)),
        check_vma=False,
    )
```

```python
import functools
import itertools

import jax
import jax.numpy as jnp
from jax import lax
from jax.experimental import pallas as pl
from jax.experimental.pallas import tpu as pltpu
from jax.sharding import Mesh
from jax.sharding import PartitionSpec as P

beta_one = 0.9
beta_two = 0.999
bias_one = 0.999973438601112
bias_two = 0.0952078528862904
epsilon = 1e-08

NAMES = ("zl", "y", "c", "x", "zh")
SIZES = {"zl": 4, "y": 4, "c": 2, "x": 4, "zh": 2}
DP = ("zl", "y", "c")
SHARD = ("x", "zh")
WIDE = jnp.float32
NARROW = jnp.bfloat16


def send(value, **shift):
    axes = tuple(name for name in NAMES if name in shift)
    sizes = [SIZES[name] for name in axes]
    flat = {at: i for i, at in enumerate(itertools.product(*map(range, sizes)))}
    pairs = [
        (i, flat[tuple((p + shift[n]) % s for p, n, s in zip(at, axes, sizes))])
        for at, i in flat.items()
    ]
    return lax.ppermute(value, axes, pairs)


def adam_step(projected_grad, first_moment, second_moment):
    new_first = beta_one * first_moment + (1.0 - beta_one) * projected_grad
    new_second = beta_two * second_moment + (1.0 - beta_two) * projected_grad * projected_grad
    direction = new_first / bias_one / (jnp.sqrt(new_second / bias_two) + epsilon)
    return (new_first, new_second, direction.astype(NARROW))


def dot(a, b, contract):
    return lax.dot_general(a, b, ((contract[:1], contract[1:]), ((), ())), preferred_element_type=WIDE)


def owner_row(slot, turned):
    cc, dy, dz, low = slot >> 8, (slot >> 6) & 3, (slot >> 4) & 3, slot & 15
    zl = (lax.axis_index("zl") + dz) & 3 if turned else dz
    y = (lax.axis_index("y") + dy) & 3
    c = (lax.axis_index("c") + cc) & 1
    return ((zl * 4 + y) * 2 + c) * 16 + low


def fold(slots, axis, *others):
    rows = slots.shape[0] // 4
    came = [send(slots[rows * s : rows * s + rows], **{axis: s}) for s in (1, 2, 3)]
    came = lax.optimization_barrier((*came, *others))[:3]
    total = slots[:rows].astype(WIDE)
    for part in came:
        total = total + part.astype(WIDE)
    return total


def spread(own, axis):
    return join([own] + [send(own, **{axis: -s}) for s in (1, 2, 3)])


def after(value, *others):
    return lax.optimization_barrier((value,) + others)[0]


def join(parts):
    rows, low = parts[0].shape[0], jnp.array(-jnp.inf, parts[0].dtype)
    padded = [
        lax.pad(part, low, ((i * rows, (len(parts) - 1 - i) * rows, 0), (0, 0, 0)))
        for i, part in enumerate(parts)
    ]
    return functools.reduce(jnp.maximum, padded)


def share_of(mine, ways):
    rows = mine.shape[0] // 2 // ways
    at = (lax.axis_index("c") * ways + lax.axis_index("y") % ways) * rows
    return lax.dynamic_slice_in_dim(mine, at, rows, 0)


def call(kernel, outs, flops, moved, scratch=(), **more):
    return pl.pallas_call(
        kernel,
        out_shape=[jax.ShapeDtypeStruct(*out) for out in outs],
        scratch_shapes=[pltpu.VMEM(*space) for space in scratch],
        cost_estimate=pl.CostEstimate(flops=flops, bytes_accessed=moved, transcendentals=0),
        compiler_params=pltpu.CompilerParams(vmem_limit_bytes=24 << 20),
        **more,
    )


def basis_kernel(mine, part, far, out):
    c, zh = lax.axis_index("c"), lax.axis_index("zh")
    slot = lax.broadcasted_iota(jnp.int32, (512, 1), 0)
    row = lax.broadcasted_iota(jnp.int32, (512, 512), 1)
    order = (row == owner_row(slot, False)).astype(WIDE).astype(NARROW)
    other = (1 - zh) * 1024
    pieces = [(mine[low : low + 256, :], zh * 1024 + low) for low in range(0, 1024, 256)]
    for some, at in ((part, other + c * 512), (far, other + (1 - c) * 512)):
        pieces += [(some[:, :512], at), (some[:, 512:], at + 256)]
    for some, at in pieces:
        moved = dot(order, some, (1, 1)).astype(NARROW)
        out[:, pl.ds(pl.multiple_of(at, 256), 256)] = moved


def project_kernel(x0, g0, xg1, xg2, xg3, basis, far, near, grads, tokens, projected):
    tokens[0:128] = x0[...]
    grads[0:128] = g0[...]
    for s, both in ((1, xg1), (2, xg2), (3, xg3)):
        tokens[128 * s : 128 * s + 128] = both[:, :2048]
        grads[128 * s : 128 * s + 128] = both[:, 2048:]
    for low in range(0, 512, 256):
        some = tokens[low : low + 256, :]
        projected[:, low : low + 256] = dot(basis[...], some, (1, 1)).astype(NARROW)
    far[...] = dot(projected[256:, :], grads[...], (1, 0)).astype(NARROW)
    near[...] = dot(projected[:256, :], grads[...], (1, 0))


def home_kernel(grads, weight, part, other, out):
    x = lax.axis_index("x")
    at = 0
    for some in (weight, part, other):
        for low in range(0, some.shape[0], 256):
            block = dot(grads[...], some[low : low + 256, :], (1, 1)).astype(NARROW)
            for s in range(4):
                out[lax.rem(x + 4 - s, 4), :, at : at + 256] = block[128 * s : 128 * s + 128]
            at += 256


def update_kernel(basis, near, far, out):
    out[...] = dot(basis[:, :256], near[...], (1, 0)) + dot(basis[:, 256:], far[...], (1, 0))


def place_kernel(blocks, out):
    c, y, zh = (lax.axis_index(name) for name in ("c", "y", "zh"))
    other = (1 - zh) * 1024
    spots = [(0, 1024, zh * 1024)]
    for cc, dy in itertools.product(range(2), range(4)):
        to = other + lax.rem(c + cc, 2) * 512 + lax.rem(y + dy, 4) * 128
        spots.append((1024 + (cc * 4 + dy) * 128, 128, to))
    for s in range(4):
        for at, size, to in spots:
            out[:, pl.ds(pl.multiple_of(2048 * s + to, 128), size)] = blocks[s, :, at : at + size]


def body(inputs, grad_out, weight, projector, first_moment, second_moment):
    x = lax.axis_index("x")

    columns = [lax.dynamic_slice_in_dim(inputs, (x + s) % 4 * 2048, 2048, 1) for s in range(4)]
    cut = [jnp.concatenate([columns[s], grad_out], 1) for s in (1, 2, 3)]
    basis_part = share_of(projector, 1)
    basis_part = jnp.concatenate([basis_part[:256], basis_part[256:]], 1)
    rows = jnp.concatenate([basis_part, share_of(weight, 4)], 0)
    cut = lax.optimization_barrier((*cut, rows))
    met = {s: send(cut[s - 1], x=s) for s in (1, 3, 2)}

    rows = send(cut[3], zh=1)
    basis_part, weight_part = rows[:256], rows[256:]
    (basis,) = call(basis_kernel, [((512, 2048), NARROW)], 1 << 20, 1 << 20)(
        projector, basis_part, send(basis_part, c=1)
    )
    quarters = [weight_part] + [send(weight_part, y=-s) for s in (1, 2, 3)]

    far, near, grads = call(
        project_kernel,
        [((256, 1024), NARROW), ((256, 1024), WIDE), ((512, 1024), NARROW)],
        4 << 30,
        10 << 20,
        [((512, 2048), NARROW), ((512, 512), NARROW)],
    )(columns[0], grad_out, met[1], met[2], met[3], basis)

    kept = near + send(far, c=1).astype(WIDE)
    kept = kept.astype(NARROW)

    kept = fold(kept, "y").astype(NARROW)
    kept = jnp.broadcast_to(kept.reshape(4, 1, 16, 1024), (4, 2, 16, 1024)).reshape(8, 16, 1024)
    kept = lax.all_to_all(kept, ("zl", "zh"), 0, 0, tiled=True)
    kept, *quarters = lax.optimization_barrier((kept, *quarters))
    kept = kept.astype(WIDE).sum(0)

    weight_part = join(quarters)
    weight_other = send(weight_part, c=1)
    (home,) = call(home_kernel, [((4, 128, 2048), NARROW)], 2 << 30, 8 << 20)(
        grads, weight, weight_part, weight_other
    )

    away = [send(kept, x=s) for s in (1, 3, 2)]
    *away, home = lax.optimization_barrier((*away, home))
    projected_grad = (kept + away[2]) + (away[0] + away[1])
    home, projected_grad = lax.optimization_barrier((home, projected_grad))
    home = lax.all_to_all(home, "x", 0, 0, tiled=True)

    new_first, new_second, direction = adam_step(projected_grad, first_moment, second_moment)

    slot = lax.broadcasted_iota(jnp.int32, (512, 512), 1)
    row = lax.broadcasted_iota(jnp.int32, (512, 512), 0)
    order = (row == owner_row(slot, True)).astype(NARROW)
    own_basis = dot(projector, order, (1, 0)).astype(NARROW)
    near = after(spread(spread(direction, "zl"), "y"), own_basis)
    far = send(near, c=1)
    (weight_update,) = call(
        update_kernel,
        [((1024, 1024), WIDE)],
        1 << 30,
        6 << 20,
        grid=(4,),
        in_specs=[
            pl.BlockSpec((256, 512), lambda i: (i, 0)),
            pl.BlockSpec((256, 1024), lambda i: (0, 0)),
            pl.BlockSpec((256, 1024), lambda i: (0, 0)),
        ],
        out_specs=[pl.BlockSpec((256, 1024), lambda i: (i, 0))],
    )(own_basis, near, far)
    (input_grad,) = call(place_kernel, [((128, 8192), NARROW)], 1 << 20, 4 << 20)(
        after(home, weight_update)
    )
    return (input_grad, weight_update, new_first, new_second)


def solution(mesh):
    fine = Mesh(mesh.devices.reshape([SIZES[name] for name in NAMES]), NAMES)
    return jax.shard_map(
        body,
        mesh=fine,
        in_specs=(
            P(DP + SHARD, None),
            P(DP + SHARD, None),
            P(SHARD, None),
            P(SHARD, None),
            P(DP, None),
            P(DP, None),
        ),
        out_specs=(P(DP + SHARD, None), P(SHARD, None), P(DP, None), P(DP, None)),
        check_vma=False,
    )
```

```python
import functools
import itertools

import jax
import jax.numpy as jnp
from jax import lax
from jax.experimental import pallas as pl
from jax.experimental.pallas import tpu as pltpu
from jax.sharding import Mesh
from jax.sharding import PartitionSpec as P

beta_one = 0.9
beta_two = 0.999
bias_one = 0.999973438601112
bias_two = 0.0952078528862904
epsilon = 1e-08

NAMES = ("zl", "y", "c", "x", "zh")
SIZES = {"zl": 4, "y": 4, "c": 2, "x": 4, "zh": 2}
DP = ("zl", "y", "c")
SHARD = ("x", "zh")
WIDE = jnp.float32
NARROW = jnp.bfloat16


def send(value, **shift):
    axes = tuple(name for name in NAMES if name in shift)
    sizes = [SIZES[name] for name in axes]
    flat = {at: i for i, at in enumerate(itertools.product(*map(range, sizes)))}
    pairs = [
        (i, flat[tuple((p + shift[n]) % s for p, n, s in zip(at, axes, sizes))])
        for at, i in flat.items()
    ]
    return lax.ppermute(value, axes, pairs)


def adam_step(projected_grad, first_moment, second_moment):
    new_first = beta_one * first_moment + (1.0 - beta_one) * projected_grad
    new_second = beta_two * second_moment + (1.0 - beta_two) * projected_grad * projected_grad
    direction = new_first / bias_one / (jnp.sqrt(new_second / bias_two) + epsilon)
    return (new_first, new_second, direction.astype(NARROW))


def dot(a, b, contract):
    return lax.dot_general(a, b, ((contract[:1], contract[1:]), ((), ())), preferred_element_type=WIDE)


def owner_row(slot, turned):
    cc, dy, dz, low = slot >> 8, (slot >> 6) & 3, (slot >> 4) & 3, slot & 15
    zl = (lax.axis_index("zl") + dz) & 3 if turned else dz
    y = (lax.axis_index("y") + dy) & 3
    c = (lax.axis_index("c") + cc) & 1
    return ((zl * 4 + y) * 2 + c) * 16 + low


def fold(slots, axis, *others):
    rows = slots.shape[0] // 4
    came = [send(slots[rows * s : rows * s + rows], **{axis: s}) for s in (1, 2, 3)]
    came = lax.optimization_barrier((*came, *others))[:3]
    total = slots[:rows].astype(WIDE)
    for part in came:
        total = total + part.astype(WIDE)
    return total


def spread(own, axis):
    return join([own] + [send(own, **{axis: -s}) for s in (1, 2, 3)])


def after(value, *others):
    return lax.optimization_barrier((value,) + others)[0]


def join(parts):
    rows, low = parts[0].shape[0], jnp.array(-jnp.inf, parts[0].dtype)
    padded = [
        lax.pad(part, low, ((i * rows, (len(parts) - 1 - i) * rows, 0), (0, 0, 0)))
        for i, part in enumerate(parts)
    ]
    return functools.reduce(jnp.maximum, padded)


def share_of(mine, ways):
    rows = mine.shape[0] // 2 // ways
    at = (lax.axis_index("c") * ways + lax.axis_index("y") % ways) * rows
    return lax.dynamic_slice_in_dim(mine, at, rows, 0)


def call(kernel, outs, flops, moved, scratch=(), **more):
    return pl.pallas_call(
        kernel,
        out_shape=[jax.ShapeDtypeStruct(*out) for out in outs],
        scratch_shapes=[pltpu.VMEM(*space) for space in scratch],
        cost_estimate=pl.CostEstimate(flops=flops, bytes_accessed=moved, transcendentals=0),
        compiler_params=pltpu.CompilerParams(vmem_limit_bytes=24 << 20),
        **more,
    )


def basis_kernel(mine, part, far, out):
    c, zh = lax.axis_index("c"), lax.axis_index("zh")
    slot = lax.broadcasted_iota(jnp.int32, (512, 1), 0)
    row = lax.broadcasted_iota(jnp.int32, (512, 512), 1)
    order = (row == owner_row(slot, False)).astype(WIDE).astype(NARROW)
    other = (1 - zh) * 1024
    pieces = [(mine[low : low + 256, :], zh * 1024 + low) for low in range(0, 1024, 256)]
    for some, at in ((part, other + c * 512), (far, other + (1 - c) * 512)):
        pieces += [(some[:, :512], at), (some[:, 512:], at + 256)]
    for some, at in pieces:
        moved = dot(order, some, (1, 1)).astype(NARROW)
        out[:, pl.ds(pl.multiple_of(at, 256), 256)] = moved


def project_kernel(x0, g0, xg1, xg2, xg3, basis, far, near, grads, tokens, projected):
    tokens[0:128] = x0[...]
    grads[0:128] = g0[...]
    for s, both in ((1, xg1), (2, xg2), (3, xg3)):
        tokens[128 * s : 128 * s + 128] = both[:, :2048]
        grads[128 * s : 128 * s + 128] = both[:, 2048:]
    for low in range(0, 512, 256):
        some = tokens[low : low + 256, :]
        projected[:, low : low + 256] = dot(basis[...], some, (1, 1)).astype(NARROW)
    far[...] = dot(projected[256:, :], grads[...], (1, 0)).astype(NARROW)
    near[...] = dot(projected[:256, :], grads[...], (1, 0))


def home_kernel(grads, weight, *refs):
    quarters, out = refs[:8], refs[8]
    x = lax.axis_index("x")
    some = [weight[low : low + 256, :] for low in range(0, 1024, 256)]
    some += [jnp.concatenate([quarters[i][...], quarters[i + 1][...]], 0) for i in range(0, 8, 2)]
    for i, rows in enumerate(some):
        block = dot(grads[...], rows, (1, 1)).astype(NARROW)
        for s in range(4):
            to = lax.rem(x + 4 - s, 4)
            out[to, :, 256 * i : 256 * i + 256] = block[128 * s : 128 * s + 128]


def update_kernel(basis, near, far, out):
    out[...] = dot(basis[:, :256], near[...], (1, 0)) + dot(basis[:, 256:], far[...], (1, 0))


def place_kernel(blocks, out):
    c, y, zh = (lax.axis_index(name) for name in ("c", "y", "zh"))
    other = (1 - zh) * 1024
    spots = [(0, 1024, zh * 1024)]
    for cc, dy in itertools.product(range(2), range(4)):
        to = other + lax.rem(c + cc, 2) * 512 + lax.rem(y + dy, 4) * 128
        spots.append((1024 + (cc * 4 + dy) * 128, 128, to))
    for s in range(4):
        for at, size, to in spots:
            out[:, pl.ds(pl.multiple_of(2048 * s + to, 128), size)] = blocks[s, :, at : at + size]


def body(inputs, grad_out, weight, projector, first_moment, second_moment):
    x = lax.axis_index("x")

    columns = [lax.dynamic_slice_in_dim(inputs, (x + s) % 4 * 2048, 2048, 1) for s in range(4)]
    cut = [jnp.concatenate([columns[s], grad_out], 1) for s in (1, 2, 3)]
    basis_part = share_of(projector, 1)
    basis_part = jnp.concatenate([basis_part[:256], basis_part[256:]], 1)
    rows = jnp.concatenate([basis_part, share_of(weight, 4)], 0)
    cut = lax.optimization_barrier((*cut, rows))
    met = {s: send(cut[s - 1], x=s) for s in (1, 3, 2)}

    rows = send(cut[3], zh=1)
    basis_part, weight_part = rows[:256], rows[256:]
    (basis,) = call(basis_kernel, [((512, 2048), NARROW)], 1 << 20, 1 << 20)(
        projector, basis_part, send(basis_part, c=1)
    )
    quarters = [weight_part] + [send(weight_part, y=-s) for s in (1, 2, 3)]

    far, near, grads = call(
        project_kernel,
        [((256, 1024), NARROW), ((256, 1024), WIDE), ((512, 1024), NARROW)],
        4 << 30,
        10 << 20,
        [((512, 2048), NARROW), ((512, 512), NARROW)],
    )(columns[0], grad_out, met[1], met[2], met[3], basis)

    kept = near + send(far, c=1).astype(WIDE)
    kept = kept.astype(NARROW)

    kept = fold(kept, "y").astype(NARROW)
    kept = jnp.broadcast_to(kept.reshape(4, 1, 16, 1024), (4, 2, 16, 1024)).reshape(8, 16, 1024)
    kept = lax.all_to_all(kept, ("zl", "zh"), 0, 0, tiled=True)
    kept, *quarters = lax.optimization_barrier((kept, *quarters))
    kept = kept.astype(WIDE).sum(0)

    quarters += [send(quarter, c=1) for quarter in quarters]
    (home,) = call(home_kernel, [((4, 128, 2048), NARROW)], 2 << 30, 8 << 20)(
        grads, weight, *quarters
    )

    away = [send(kept, x=s) for s in (1, 3, 2)]
    *away, home = lax.optimization_barrier((*away, home))
    projected_grad = (kept + away[2]) + (away[0] + away[1])
    home, projected_grad = lax.optimization_barrier((home, projected_grad))
    home = lax.all_to_all(home, "x", 0, 0, tiled=True)

    new_first, new_second, direction = adam_step(projected_grad, first_moment, second_moment)

    slot = lax.broadcasted_iota(jnp.int32, (512, 512), 1)
    row = lax.broadcasted_iota(jnp.int32, (512, 512), 0)
    order = (row == owner_row(slot, True)).astype(NARROW)
    own_basis = dot(projector, order, (1, 0)).astype(NARROW)
    near = after(spread(spread(direction, "zl"), "y"), own_basis)
    far = send(near, c=1)
    (weight_update,) = call(
        update_kernel,
        [((1024, 1024), WIDE)],
        1 << 30,
        6 << 20,
        grid=(4,),
        in_specs=[
            pl.BlockSpec((256, 512), lambda i: (i, 0)),
            pl.BlockSpec((256, 1024), lambda i: (0, 0)),
            pl.BlockSpec((256, 1024), lambda i: (0, 0)),
        ],
        out_specs=[pl.BlockSpec((256, 1024), lambda i: (i, 0))],
    )(own_basis, near, far)
    (input_grad,) = call(place_kernel, [((128, 8192), NARROW)], 1 << 20, 4 << 20)(
        after(home, weight_update)
    )
    return (input_grad, weight_update, new_first, new_second)


def solution(mesh):
    fine = Mesh(mesh.devices.reshape([SIZES[name] for name in NAMES]), NAMES)
    return jax.shard_map(
        body,
        mesh=fine,
        in_specs=(
            P(DP + SHARD, None),
            P(DP + SHARD, None),
            P(SHARD, None),
            P(SHARD, None),
            P(DP, None),
            P(DP, None),
        ),
        out_specs=(P(DP + SHARD, None), P(SHARD, None), P(DP, None), P(DP, None)),
        check_vma=False,
    )
```
